256 devices in a mesh: pop: 8 (over x, core), mp: 32 (over z, y).
Axes of the slice: x: 4, y: 4, z: 8, core: 2. Of those that a mesh axis runs over, the one named last changes fastest.
Arguments:
- inputs: bfloat16 [8192, 4096], P('pop', 'mp'), may hold values from -6 to 6
- mix_gain: float32 [4096], P('mp'), may hold values from 0 to 1
- key_weight: bfloat16 [4096, 16384], P(None, 'mp'), may hold values from -0.09375 to 0.09375
- value_weight: bfloat16 [16384, 4096], P('mp'), may hold values from -0.046875 to 0.046875
- key_left: bfloat16 [2048, 4096], P('pop'), may hold values from -6 to 6
- key_right: bfloat16 [2048, 16384], P('pop', 'mp'), may hold values from -6 to 6
- value_left: bfloat16 [2048, 16384], P('pop', 'mp'), may hold values from -6 to 6
- value_right: bfloat16 [2048, 4096], P('pop'), may hold values from -6 to 6
- fitness: float32 [2048], P('pop'), may hold values from -9 to 9
Outputs:
- outputs: bfloat16 [8192, 4096], P('pop', 'mp')
- key_update: float32 [4096, 16384], P('pop', 'mp')
- value_update: float32 [16384, 4096], P('mp', 'pop')
The draws below stay inside these ranges and needn't reach their ends.
All inputs are finite; a program needn't handle non-finite values.
Results may differ from the reference program's by a relative error of at most 0.04.
Values may be sent and summed in bfloat16 or wider, within the bound.
No kernel may reach another device: no remote copies, remote signals or barrier semaphores. Data moves between devices by JAX's collectives and lax.ppermute only.
A program may use at most 128 MiB of HBM per device.

```python
import math
import jax
import jax.numpy as jnp
from jax import lax

D = 4096
FF = 16384
TOKS = 4
MEMBERS = 2048
TOKENS = 8192
N_MP = 32


def draw_fitness(key, part):
    key = jax.random.fold_in(key, 11)
    position = jnp.arange(MEMBERS, dtype=jnp.float32)
    growth = 1.0 + 2.0 * position / MEMBERS
    values = jax.random.truncated_normal(key, -3.0, 3.0, (MEMBERS,), jnp.float32) * growth
    return values.astype(jnp.float32)


def steps_of(stream_key, dims, pieces, smallest, high):
    loudness = 1.0
    for dim, parts in pieces:
        heights = jax.random.uniform(jax.random.fold_in(jax.random.fold_in(stream_key, 6), dim), (parts,), jnp.float32, smallest / len(pieces), high / len(pieces))
        loudness = loudness * jnp.repeat(jnp.exp(heights), dims[dim] // parts).reshape((-1,) + (1,) * (len(dims) - 1 - dim))
    return loudness


def scatter_about(key, extent, width, reach, pieces=(), kind=jnp.bfloat16):
    array = jax.random.normal(key, extent, jnp.float32) * width
    if len(pieces) > 0:
        array = steps_of(key, extent, pieces, -0.22, 0.18) * array
    return jnp.clip(array, min=-reach, max=reach).astype(kind)


def setup_inputs(seed: int = 0) -> dict:
    key_of = jax.random.split(jax.random.key(seed), 10)
    return {
        "inputs": scatter_about(key_of[0], (TOKENS, D), 1.0, 6.0, ((0, 8), (1, 32))),
        "mix_gain": jnp.clip(1.0 * jax.random.uniform(key_of[1], (D,), jnp.float32) ** steps_of(key_of[1], (D,), ((0, 32),), -0.2, 0.2), 0.0, 1.0),
        "key_weight": scatter_about(key_of[2], (D, FF), D ** -0.5, 0.09375, ((1, 32),)),
        "value_weight": scatter_about(key_of[3], (FF, D), FF ** -0.5, 0.046875, ((0, 32),)),
        "key_left": scatter_about(key_of[4], (MEMBERS, D), 1.0, 6.0, ((0, 8),)),
        "key_right": scatter_about(key_of[5], (MEMBERS, FF), 1.0, 6.0, ((0, 8), (1, 32))),
        "value_left": scatter_about(key_of[6], (MEMBERS, FF), 1.0, 6.0, ((0, 8), (1, 32))),
        "value_right": scatter_about(key_of[7], (MEMBERS, D), 1.0, 6.0, ((0, 8),)),
        "fitness": draw_fitness(jax.random.fold_in(key_of[9], 71), 0),
    }


def reference(inputs, mix_gain, key_weight, value_weight, key_left, key_right, value_left, value_right, fitness):
    tokens3 = inputs.astype(jnp.float32).reshape(MEMBERS, TOKS, D)
    previous = jnp.concatenate([jnp.zeros((MEMBERS, 1, D), jnp.float32), tokens3[:, :-1]], axis=1)
    shifted = (tokens3 + mix_gain * (previous - tokens3)).astype(jnp.bfloat16)
    base = jnp.dot(shifted.reshape(TOKENS, D), key_weight, preferred_element_type=jnp.float32)
    left_dots = jnp.einsum('mtd,md->mt', shifted.astype(jnp.float32), key_left.astype(jnp.float32))
    hidden = base.reshape(MEMBERS, TOKS, FF) + left_dots[..., None] * key_right.astype(jnp.float32)[:, None, :] / math.sqrt(D)
    keyed = (jnp.maximum(hidden, 0.0) ** 2).astype(jnp.bfloat16)
    block_width = FF // N_MP
    keyed_blocks = keyed.reshape(TOKENS, N_MP, block_width).transpose(1, 0, 2)
    left_blocks = value_left.reshape(MEMBERS, N_MP, block_width).transpose(1, 0, 2)
    weight_blocks = value_weight.reshape(N_MP, block_width, D)
    right_scaled = value_right.astype(jnp.float32) / math.sqrt(FF)

    def add_block(total, items):
        keyed_part, left_part, weight_part = items
        partial_value = jnp.dot(keyed_part, weight_part, preferred_element_type=jnp.float32)
        dots = jnp.einsum('mtf,mf->mt', keyed_part.reshape(MEMBERS, TOKS, block_width).astype(jnp.float32), left_part.astype(jnp.float32))
        partial_value = partial_value.reshape(MEMBERS, TOKS, D) + dots[..., None] * right_scaled[:, None, :]
        rounded = lax.optimization_barrier(partial_value.reshape(TOKENS, D).astype(jnp.bfloat16))
        return (total + rounded.astype(jnp.float32), None)
    total, unused = lax.scan(add_block, jnp.zeros((TOKENS, D), jnp.float32), (keyed_blocks, left_blocks, weight_blocks))
    outputs = total.astype(jnp.bfloat16)
    total_fit = jnp.sum(fitness)
    squares = jnp.sum(fitness * fitness)
    mean = total_fit / MEMBERS
    spread = squares / MEMBERS - mean * mean
    scores = (fitness - mean) / jnp.sqrt(spread + 1e-05)
    scaled_right = (scores[:, None] * key_right.astype(jnp.float32)).astype(jnp.bfloat16)
    scaled_value = (scores[:, None] * value_right.astype(jnp.float32)).astype(jnp.bfloat16)
    key_update = jnp.dot(key_left.T, scaled_right, preferred_element_type=jnp.float32) / math.sqrt(MEMBERS)
    value_update = jnp.dot(value_left.T, scaled_value, preferred_element_type=jnp.float32) / math.sqrt(MEMBERS)
    return (outputs, key_update, value_update)
```

```python
import functools
import math

import jax
import jax.numpy as jnp
from jax import lax
from jax.experimental import pallas as pl
from jax.experimental.pallas import tpu as pltpu
from jax.sharding import PartitionSpec as P

TOKS = 4
NZ = 8
NY = 4
CUT = 10
OFFSETS = (4, 3, -3, 2, -2, 1, -1, 0)
F32 = jnp.float32
BF16 = jnp.bfloat16


def along_z(x, step):
    perm = [(z * NY + y, (z + step) % NZ * NY + y) for z in range(NZ) for y in range(NY)]
    return lax.ppermute(x, "mp", perm)


def along_y(x, step):
    perm = [(z * NY + y, z * NY + (y + step) % NY) for z in range(NZ) for y in range(NY)]
    return lax.ppermute(x, "mp", perm)


def after(x, *earlier):
    return lax.optimization_barrier((x, *earlier))[0]


def ring_scatter(own, count, move, split=True):
    far = own(count // 2).astype(BF16)
    half = far.shape[0] // 2
    if split:
        up, down = yield move(far[:half], 1), move(far[half:], -1)
    else:
        up, down = yield move(far, 1), None
    for step in range(count // 2 - 1, 0, -1):
        ahead, behind = own(step).astype(F32), own(-step).astype(F32)
        if step < count // 2 - 1:
            ahead, behind = ahead + up.astype(F32), behind + down.astype(F32)
        elif split:
            ahead = jnp.concatenate([ahead[:half] + up.astype(F32), ahead[half:]], axis=0)
            behind = jnp.concatenate([behind[:half], behind[half:] + down.astype(F32)], axis=0)
        else:
            ahead = ahead + up.astype(F32)
        up, down = yield move(ahead.astype(BF16), 1), move(behind.astype(BF16), -1)
    yield own(0).astype(F32) + up.astype(F32) + down.astype(F32)


def gather_z(x):
    got = {0: x}
    up = down = x
    for step in range(1, NZ // 2):
        up, down = yield along_z(up, 1), along_z(down, -1)
        got[-step], got[step] = up, down
    half = x.shape[0] // 2
    up, down = along_z(up[:half], 1), along_z(down[half:], -1)
    got[NZ // 2] = jnp.concatenate([up, down], axis=0)
    yield got


def order_kernel(me_ref, *refs):
    *blocks, out = refs
    width = blocks[0].shape[1]
    for k, block in enumerate(blocks):
        place = lax.rem(me_ref[0] + k, NY) * width
        out[:, pl.ds(pl.multiple_of(place, width), width)] = block[...]


def in_order(blocks, me):
    rows, width = blocks[0].shape
    return pl.pallas_call(
        order_kernel,
        in_specs=[pl.BlockSpec(memory_space=pltpu.SMEM)]
        + [pl.BlockSpec(memory_space=pltpu.VMEM)] * NY,
        out_specs=pl.BlockSpec(memory_space=pltpu.VMEM),
        out_shape=jax.ShapeDtypeStruct((rows, NY * width), BF16),
        cost_estimate=pl.CostEstimate(
            flops=0, bytes_accessed=4 * NY * rows * width, transcendentals=0
        ),
        name="in_order",
    )(me.reshape(1).astype(jnp.int32), *blocks)


def scatter_y(own):
    total = own(0)
    for k in (2, 1, -1):
        total = total + along_y(own(k).astype(BF16), k).astype(F32)
    return total


def dot(a, b):
    return jnp.dot(a, b, preferred_element_type=F32)


def total_over_pop(x):
    for bit in (1, 2, 4):
        x = x + lax.ppermute(x, "pop", [(i, i ^ bit) for i in range(8)])
    return x


def columns(ref, first, step, count, width):
    parts = [
        ref[:, pl.ds(pl.multiple_of((first + step * n) * width, width), width)]
        for n in range(count)
    ]
    return jnp.concatenate(parts, axis=1)


def hidden_kernel(scale, members, order_ref, *refs):
    *blocks, weight, left, right, value_left, keyed_ref, value_dots_ref = refs
    deep = blocks[0].shape[1]
    lanes = value_dots_ref.shape[1]
    base = products = 0.0
    for n, block in enumerate(blocks):
        place = pl.ds(pl.multiple_of(order_ref[n] * deep, deep), deep)
        base = base + dot(block[...], weight[place, :])
        terms = block[...].astype(F32) * left[members, place].astype(F32)
        products = products + sum(terms[:, at : at + lanes] for at in range(0, deep, lanes))
    left_dots = jnp.sum(products, axis=1, keepdims=True)
    hidden = jnp.maximum(base + left_dots * (right[members, :].astype(F32) * scale), 0.0)
    keyed = (hidden * hidden).astype(BF16)
    keyed_ref[...] = keyed
    sums = jnp.sum(keyed.astype(F32) * value_left[members, :].astype(F32), axis=1, keepdims=True)
    value_dots_ref[...] = jnp.broadcast_to(sums, value_dots_ref.shape)


def hidden(blocks, order, members, key_weight, key_left, key_right, value_left):
    count = members.stop - members.start
    units = key_weight.shape[1]
    rows, deep = blocks[0].shape
    whole = lambda x: pl.BlockSpec(x.shape, lambda i, order: (0, 0))
    part = lambda wide: pl.BlockSpec((count, wide), lambda i, order: (i, 0))
    rest = (key_weight, key_left, key_right, value_left)
    return pl.pallas_call(
        functools.partial(hidden_kernel, 1.0 / math.sqrt(key_left.shape[1]), members),
        grid_spec=pltpu.PrefetchScalarGridSpec(
            num_scalar_prefetch=1,
            grid=(TOKS,),
            in_specs=[part(deep) for _ in blocks] + [whole(x) for x in rest],
            out_specs=[part(units), part(128)],
        ),
        out_shape=[
            jax.ShapeDtypeStruct((rows, units), BF16),
            jax.ShapeDtypeStruct((rows, 128), F32),
        ],
        compiler_params=pltpu.CompilerParams(vmem_limit_bytes=48 * 2**20),
        cost_estimate=pl.CostEstimate(
            flops=2 * rows * key_weight.size,
            bytes_accessed=2 * (rows * key_left.shape[1] + key_weight.size + key_left.size),
            transcendentals=0,
        ),
        name="hidden",
    )(order, *blocks, *rest)


def partial_terms(keyed, value_dots, weight, rights, scale):
    terms = dot(keyed[...], weight)
    rights = rights.astype(F32) * scale
    count = rights.shape[0]
    parts = []
    for token in range(TOKS):
        rows = slice(token * count, (token + 1) * count)
        parts.append((terms[rows] + value_dots[rows, :1] * rights).astype(BF16))
    return parts


def partial_z_kernel(scale, members, order_ref, keyed, value_dots, weight, right, out):
    count = members.stop - members.start
    parts = partial_terms(keyed, value_dots, weight[...], right[members, :], scale)
    for token, part in enumerate(parts):
        out[0, token * count : (token + 1) * count, :] = part


def partial_y_kernel(scale, members, order_ref, keyed, value_dots, weight, right, out):
    y = order_ref[pl.program_id(0)]
    count = members.stop - members.start
    feats = out.shape[2] // NZ
    picks = [
        pl.ds(pl.multiple_of((z * NY + y) * feats, feats), feats) for z in range(NZ)
    ]
    weights = jnp.concatenate([weight[:, pick] for pick in picks], axis=1)
    rights = jnp.concatenate([right[members, pick] for pick in picks], axis=1)
    parts = partial_terms(keyed, value_dots, weights, rights, scale)
    for token, part in enumerate(parts):
        out[0, token * count : (token + 1) * count, :] = part


def partial(keyed, value_dots, order, members, weight, right, scale, by_y):
    rows, units = keyed.shape
    width = weight.shape[1]
    whole = lambda x: pl.BlockSpec(x.shape, lambda i, order: (0, 0))
    steps = NY if by_y else NZ
    if by_y:
        kernel = partial_y_kernel
        weight_specs = [whole(weight), whole(right)]
    else:
        kernel = partial_z_kernel
        weight_specs = [
            pl.BlockSpec((x.shape[0], width // NZ), lambda i, order: (0, order[i]))
            for x in (weight, right)
        ]
    shape = (steps, rows, width // steps)
    out_spec = pl.BlockSpec((1,) + shape[1:], lambda i, order: (i, 0, 0))
    return pl.pallas_call(
        functools.partial(kernel, scale, members),
        grid_spec=pltpu.PrefetchScalarGridSpec(
            num_scalar_prefetch=1,
            grid=(steps,),
            in_specs=[whole(keyed), whole(value_dots)] + weight_specs,
            out_specs=out_spec,
        ),
        out_shape=jax.ShapeDtypeStruct(shape, BF16),
        compiler_params=pltpu.CompilerParams(vmem_limit_bytes=48 * 2**20),
        cost_estimate=pl.CostEstimate(
            flops=2 * rows * units * width,
            bytes_accessed=2 * width * (rows + units),
            transcendentals=0,
        ),
        name="partial",
    )(order, keyed, value_dots, weight, right)


def shards(
    inputs,
    mix_gain,
    key_weight,
    value_weight,
    key_left,
    key_right,
    value_left,
    value_right,
    fitness,
):
    members, width = key_left.shape
    feats = inputs.shape[1]
    hidden_units = key_weight.shape[1]
    all_members = members * lax.axis_size("pop")
    all_hidden = hidden_units * lax.axis_size("mp")
    member_scale = math.sqrt(all_members)
    me = lax.axis_index("mp")
    my_z, my_y = me // NY, me % NY
    tokens = inputs.reshape(members, TOKS, feats).transpose(1, 0, 2).astype(F32)
    previous = jnp.concatenate([jnp.zeros_like(tokens[:1]), tokens[:-1]], axis=0)
    shifted = (tokens + mix_gain * (previous - tokens)).astype(BF16)
    barrier = lax.optimization_barrier
    cut = members * CUT // 16
    first, second = slice(0, cut), slice(cut, members)
    second_all = lax.all_gather(shifted[:, second].reshape(-1, feats), "mp", axis=1, tiled=True)
    mine = shifted[:, first].reshape(-1, feats)
    first_block = in_order([mine] + [along_y(mine, -k) for k in (1, 2, 3)], my_y)
    steps = gather_z(first_block)
    step = next(steps)

    pair = after(fitness, first_block).reshape(1, members)
    pair = jnp.concatenate([pair, pair * pair], axis=0)
    sums = total_over_pop(jnp.sum(pair, axis=1, keepdims=True)) / all_members
    mean, square = sums[:1], sums[1:]
    scores = (fitness.reshape(1, members) - mean) / jnp.sqrt(square - mean * mean + 1e-05)
    scores = scores.reshape(members)

    step, scores = barrier((step, scores))
    step = steps.send(step)

    scaled_right = (scores[:, None] * key_right.astype(F32)).astype(BF16)
    scaled_value = (scores[:, None] * value_right.astype(F32)).astype(BF16)
    member_dims = (((0,), (0,)), ((), ()))
    key_terms = lax.dot_general(
        key_left, scaled_right, member_dims, preferred_element_type=F32
    )
    value_terms = lax.dot_general(
        value_left, scaled_value, member_dims, preferred_element_type=F32
    )
    key_terms = (key_terms / member_scale).astype(BF16)
    value_terms = (value_terms / member_scale).astype(BF16)

    step, key_terms, value_terms = barrier((step, key_terms, value_terms))
    step = barrier(steps.send(step))
    first_got = steps.send(step)
    key_update = lax.psum_scatter(key_terms, "pop", scatter_dimension=0, tiled=True)
    value_update = lax.psum_scatter(value_terms, "pop", scatter_dimension=1, tiled=True)

    weights = (key_weight, key_left, key_right, value_left)
    order = ((my_z + jnp.array(OFFSETS, jnp.int32)) % NZ).astype(jnp.int32)
    first_keyed, first_dots = hidden([first_got[k] for k in OFFSETS], order, first, *weights)
    second_keyed, second_dots = hidden(
        [after(second_all, first_keyed)], jnp.zeros(1, jnp.int32), second, *weights
    )

    scale = 1.0 / math.sqrt(all_hidden)

    values = (value_weight, value_right, scale)
    first_terms = partial(first_keyed, first_dots, order, first, *values, by_y=False)
    order = ((my_y + jnp.array((2, 1, -1, 0), jnp.int32)) % NY).astype(jnp.int32)
    second_terms = partial(second_keyed, second_dots, order, second, *values, by_y=True)

    def columns(x, index):
        return lax.dynamic_slice_in_dim(x, index * feats, feats, axis=1)

    key_update, value_update = key_update.astype(F32), value_update.astype(F32)
    first_steps = ring_scatter(lambda k: first_terms[OFFSETS.index(k)], NZ, along_z)
    second_steps = ring_scatter(lambda k: second_terms[(2, 1, -1, 0).index(k)], NY, along_y)
    first, second = next(first_steps), next(second_steps)
    first, second_next = first_steps.send(first), second_steps.send(second)
    first = first_steps.send(after(first, second))
    first, key_update, value_update, second = lax.optimization_barrier(
        (first, key_update, value_update, second_next)
    )
    first = first_steps.send(first)
    second_sum = second_steps.send(second)
    second_steps = ring_scatter(
        lambda k: columns(second_sum, (my_z + k) % NZ), NZ, along_z, split=False
    )
    second = next(second_steps)
    first_sum = first_steps.send(first)
    second = after(second, *first)
    first_out = scatter_y(lambda k: columns(first_sum, (my_y + k) % NY))
    second = second_steps.send(second)
    second = second_steps.send(second)
    second = second_steps.send(second)
    second_out = second_steps.send(second)
    outputs = jnp.concatenate(
        [x.reshape(TOKS, -1, feats) for x in (first_out, second_out)], axis=1
    )
    outputs = outputs.astype(BF16).transpose(1, 0, 2).reshape(members * TOKS, feats)
    return outputs, key_update, value_update


def solution(mesh):
    placed = (
        P("pop", "mp"),
        P("mp"),
        P(None, "mp"),
        P("mp", None),
        P("pop", None),
        P("pop", "mp"),
        P("pop", "mp"),
        P("pop", None),
        P("pop"),
    )
    return jax.shard_map(
        shards,
        mesh=mesh,
        in_specs=placed,
        out_specs=(P("pop", "mp"), P("pop", "mp"), P("mp", "pop")),
        check_vma=False,
    )
```

```python
import functools
import math

import jax
import jax.numpy as jnp
from jax import lax
from jax.experimental import pallas as pl
from jax.experimental.pallas import tpu as pltpu
from jax.sharding import PartitionSpec as P

TOKS = 4
NZ = 8
NY = 4
CUT = 10
ALONG_Z = [[z * NY + y for z in range(NZ)] for y in range(NY)]
ALONG_Y = [[z * NY + y for y in range(NY)] for z in range(NZ)]
OFFSETS = (4, 3, -3, 2, -2, 1, -1, 0)
F32 = jnp.float32
BF16 = jnp.bfloat16


def along_z(x, step):
    perm = [(z * NY + y, (z + step) % NZ * NY + y) for z in range(NZ) for y in range(NY)]
    return lax.ppermute(x, "mp", perm)


def along_y(x, step):
    perm = [(z * NY + y, z * NY + (y + step) % NY) for z in range(NZ) for y in range(NY)]
    return lax.ppermute(x, "mp", perm)


def after(x, *earlier):
    return lax.optimization_barrier((x, *earlier))[0]


def ring_scatter(far, own, count, move):
    half = far[0].shape[0]
    up, down = yield move(far[0], 1), move(far[1], -1)
    for step in range(count // 2 - 1, 0, -1):
        ahead, behind = own(step).astype(F32), own(-step).astype(F32)
        if step < count // 2 - 1:
            ahead, behind = ahead + up.astype(F32), behind + down.astype(F32)
        else:
            ahead = jnp.concatenate([ahead[:half] + up.astype(F32), ahead[half:]], axis=0)
            behind = jnp.concatenate([behind[:half], behind[half:] + down.astype(F32)], axis=0)
        up, down = yield move(ahead.astype(BF16), 1), move(behind.astype(BF16), -1)
    yield own(0).astype(F32) + up.astype(F32) + down.astype(F32)


def gather_z(x):
    got = {0: x}
    up = down = x
    for step in range(1, NZ // 2):
        up, down = yield along_z(up, 1), along_z(down, -1)
        got[-step], got[step] = up, down
    got[NZ // 2] = along_z(up, 1)
    yield got


def order_kernel(me_ref, *refs):
    *blocks, out = refs
    width = blocks[0].shape[1]
    for k, block in enumerate(blocks):
        place = lax.rem(me_ref[0] + k, NY) * width
        out[:, pl.ds(pl.multiple_of(place, width), width)] = block[...]


def in_order(blocks, me):
    rows, width = blocks[0].shape
    return pl.pallas_call(
        order_kernel,
        in_specs=[pl.BlockSpec(memory_space=pltpu.SMEM)]
        + [pl.BlockSpec(memory_space=pltpu.VMEM)] * NY,
        out_specs=pl.BlockSpec(memory_space=pltpu.VMEM),
        out_shape=jax.ShapeDtypeStruct((rows, NY * width), BF16),
        cost_estimate=pl.CostEstimate(
            flops=0, bytes_accessed=4 * NY * rows * width, transcendentals=0
        ),
        name="in_order",
    )(me.reshape(1).astype(jnp.int32), *blocks)


def scatter_straight(own, offsets, move):
    return [move(own(k).astype(BF16), k) for k in offsets]


def total(own, sent):
    return sum((x.astype(F32) for x in sent), own)


def dot(a, b):
    return jnp.dot(a, b, preferred_element_type=F32)


def total_over_pop(x):
    for bit in (1, 2, 4):
        x = x + lax.ppermute(x, "pop", [(i, i ^ bit) for i in range(8)])
    return x


def columns(ref, first, step, count, width):
    parts = [
        ref[:, pl.ds(pl.multiple_of((first + step * n) * width, width), width)]
        for n in range(count)
    ]
    return jnp.concatenate(parts, axis=1)


def sums_kernel(members, carried, order_ref, *refs):
    *blocks, weight, left, base_ref, products_ref = refs
    base = products = 0.0
    if carried:
        *blocks, base_in, products_in = blocks
        base, products = base_in[...], products_in[...]
    lanes = products_ref.shape[1]
    for n, block in enumerate(blocks):
        if len(block.shape) == 2:
            tokens = block[...]
        else:
            tokens = jnp.concatenate(
                [block[y, z] for z in range(NZ) for y in range(NY)], axis=1
            )
        deep = tokens.shape[1]
        place = pl.ds(0, deep)
        if len(blocks) > 1:
            place = pl.ds(pl.multiple_of(order_ref[n] * deep, deep), deep)
        base = base + dot(tokens, weight[place, :])
        terms = tokens.astype(F32) * left[members, place].astype(F32)
        products = products + sum(terms[:, at : at + lanes] for at in range(0, deep, lanes))
    base_ref[...] = base
    products_ref[...] = products


def hidden_kernel(scale, members, carried, order_ref, *refs):
    *given, right, value_left, keyed_ref, value_dots_ref, base, products = refs
    sums_kernel(members, carried, order_ref, *given, base, products)
    left_dots = jnp.sum(products[...], axis=1, keepdims=True)
    hidden = base[...] + left_dots * (right[members, :].astype(F32) * scale)
    hidden = jnp.maximum(hidden, 0.0)
    keyed = (hidden * hidden).astype(BF16)
    keyed_ref[...] = keyed
    sums = jnp.sum(keyed.astype(F32) * value_left[members, :].astype(F32), axis=1, keepdims=True)
    value_dots_ref[...] = jnp.broadcast_to(sums, value_dots_ref.shape)


def hidden(blocks, order, members, weights, carried=(), last=True):
    key_weight, key_left, key_right, value_left = weights
    count = members.stop - members.start
    units = key_weight.shape[1]
    rows, deep = count * TOKS, blocks[0].shape[-1]
    whole = lambda x: pl.BlockSpec(x.shape, lambda i, order: (0, 0))
    part = lambda wide: pl.BlockSpec((count, wide), lambda i, order: (i, 0))
    if len(blocks[0].shape) == 2:
        specs = [part(deep) for _ in blocks]
    else:
        specs = [pl.BlockSpec((NY, NZ, count, deep), lambda i, order: (0, 0, i, 0))]
        deep = deep * NY * NZ
    specs += [part(x.shape[1]) for x in carried]
    if len(blocks) > 1:
        specs += [whole(key_weight), whole(key_left)]
    else:
        specs += [
            pl.BlockSpec((deep, units), lambda i, order: (order[0], 0)),
            pl.BlockSpec((key_left.shape[0], deep), lambda i, order: (0, order[0])),
        ]
    given = [*blocks, *carried, key_weight, key_left]
    if last:
        kernel = functools.partial(
            hidden_kernel, 1.0 / math.sqrt(key_left.shape[1]), members, bool(carried)
        )
        given, specs = given + [key_right, value_left], specs + [whole(key_right), whole(value_left)]
        scratch = [pltpu.VMEM((count, units), F32), pltpu.VMEM((count, 128), F32)]
    else:
        kernel = functools.partial(sums_kernel, members, bool(carried))
        scratch = []
    features = deep * len(blocks)
    return pl.pallas_call(
        kernel,
        grid_spec=pltpu.PrefetchScalarGridSpec(
            num_scalar_prefetch=1,
            grid=(TOKS,),
            in_specs=specs,
            out_specs=[part(units), part(128)],
            scratch_shapes=scratch,
        ),
        out_shape=[
            jax.ShapeDtypeStruct((rows, units), BF16 if last else F32),
            jax.ShapeDtypeStruct((rows, 128), F32),
        ],
        compiler_params=pltpu.CompilerParams(vmem_limit_bytes=48 * 2**20),
        cost_estimate=pl.CostEstimate(
            flops=2 * rows * features * units,
            bytes_accessed=2 * features * (rows + units + key_left.shape[0]) + 4 * rows * units,
            transcendentals=0,
        ),
        name="hidden",
    )(order, *given)


def partial_terms(keyed, value_dots, weight, rights, scale):
    terms = dot(keyed[...], weight)
    rights = rights.astype(F32) * scale
    count = rights.shape[0]
    parts = []
    for token in range(TOKS):
        rows = slice(token * count, (token + 1) * count)
        parts.append((terms[rows] + value_dots[rows, :1] * rights).astype(BF16))
    return parts


def partial_z_kernel(scale, members, order_ref, keyed, value_dots, weight, right, *outs):
    count = members.stop - members.start
    parts = partial_terms(keyed, value_dots, weight[...], right[members, :], scale)
    for token, part in enumerate(parts):
        out = outs[token * len(outs) // TOKS]
        at = token % (TOKS // len(outs)) * count
        out[0, at : at + count, :] = part


def partial_y_kernel(scale, members, order_ref, keyed, value_dots, weight, right, out):
    y = order_ref[pl.program_id(0)]
    count = members.stop - members.start
    feats = out.shape[2] // NZ
    picks = [
        pl.ds(pl.multiple_of((z * NY + y) * feats, feats), feats) for z in range(NZ)
    ]
    weights = jnp.concatenate([weight[:, pick] for pick in picks], axis=1)
    rights = jnp.concatenate([right[members, pick] for pick in picks], axis=1)
    parts = partial_terms(keyed, value_dots, weights, rights, scale)
    for token, part in enumerate(parts):
        out[0, token * count : (token + 1) * count, :] = part


def partial(keyed, value_dots, order, members, weight, right, scale, by_y=False, parts=1):
    rows, units = keyed.shape
    width = weight.shape[1]
    whole = lambda x: pl.BlockSpec(x.shape, lambda i, order: (0, 0))
    ring = NY if by_y else NZ
    if by_y:
        kernel = partial_y_kernel
        weight_specs = [whole(weight), whole(right)]
    else:
        kernel = partial_z_kernel
        weight_specs = [
            pl.BlockSpec((x.shape[0], width // NZ), lambda i, order: (0, order[i]))
            for x in (weight, right)
        ]
    shape = (len(order), rows // parts, width // ring)
    return pl.pallas_call(
        functools.partial(kernel, scale, members),
        grid_spec=pltpu.PrefetchScalarGridSpec(
            num_scalar_prefetch=1,
            grid=(len(order),),
            in_specs=[whole(keyed), whole(value_dots)] + weight_specs,
            out_specs=[pl.BlockSpec((1,) + shape[1:], lambda i, order: (i, 0, 0))] * parts,
        ),
        out_shape=[jax.ShapeDtypeStruct(shape, BF16)] * parts,
        compiler_params=pltpu.CompilerParams(vmem_limit_bytes=48 * 2**20),
        cost_estimate=pl.CostEstimate(
            flops=2 * rows * units * len(order) * (width // ring),
            bytes_accessed=2 * len(order) * (width // ring) * (rows + units),
            transcendentals=0,
        ),
        name="partial",
    )(order, keyed, value_dots, weight, right)


def shards(
    inputs,
    mix_gain,
    key_weight,
    value_weight,
    key_left,
    key_right,
    value_left,
    value_right,
    fitness,
):
    members, width = key_left.shape
    feats = inputs.shape[1]
    hidden_units = key_weight.shape[1]
    all_members = members * lax.axis_size("pop")
    all_hidden = hidden_units * lax.axis_size("mp")
    member_scale = math.sqrt(all_members)
    me = lax.axis_index("mp")
    my_z, my_y = me // NY, me % NY
    tokens = inputs.reshape(members, TOKS, feats).transpose(1, 0, 2).astype(F32)
    previous = jnp.concatenate([jnp.zeros_like(tokens[:1]), tokens[:-1]], axis=0)
    shifted = (tokens + mix_gain * (previous - tokens)).astype(BF16)
    barrier = lax.optimization_barrier
    cut = members * CUT // 16
    first, second = slice(0, cut), slice(cut, members)
    latter = shifted[:, members // 2 :].reshape(-1, feats)
    second_z = lax.all_gather(latter, "mp", axis_index_groups=ALONG_Z)
    mine = shifted[:, first].reshape(-1, feats)
    first_block = in_order([mine] + [along_y(mine, -k) for k in (1, 2, 3)], my_y)
    steps = gather_z(first_block)
    step = next(steps)

    pair = after(fitness, first_block).reshape(1, members)
    pair = jnp.concatenate([pair, pair * pair], axis=0)
    sums = total_over_pop(jnp.sum(pair, axis=1, keepdims=True)) / all_members
    mean, square = sums[:1], sums[1:]
    scores = (fitness.reshape(1, members) - mean) / jnp.sqrt(square - mean * mean + 1e-05)
    scores = scores.reshape(members)

    step, scores = barrier((step, scores))
    step = steps.send(step)

    scaled_right = (scores[:, None] * key_right.astype(F32)).astype(BF16)
    scaled_value = (scores[:, None] * value_right.astype(F32)).astype(BF16)
    member_dims = (((0,), (0,)), ((), ()))
    key_terms = lax.dot_general(
        key_left, scaled_right, member_dims, preferred_element_type=F32
    )
    value_terms = lax.dot_general(
        value_left, scaled_value, member_dims, preferred_element_type=F32
    )
    key_terms = (key_terms / member_scale).astype(BF16)
    value_terms = (value_terms / member_scale).astype(BF16)

    step, key_terms, value_terms = barrier((step, key_terms, value_terms))
    second_z = after(second_z, *step).reshape(NZ, TOKS, -1, feats)[:, :, cut - members // 2 :]
    second_all = lax.all_gather(
        second_z.reshape(NZ, -1, feats), "mp", axis_index_groups=ALONG_Y
    )
    step = barrier(steps.send(step))
    first_got = steps.send(step)
    order = ((my_z + jnp.array(OFFSETS, jnp.int32)) % NZ).astype(jnp.int32)
    key_update = lax.psum_scatter(key_terms, "pop", scatter_dimension=0, tiled=True)
    value_update = lax.psum_scatter(value_terms, "pop", scatter_dimension=1, tiled=True)

    weights = (key_weight, key_left, key_right, value_left)
    carried = hidden([first_got[k] for k in OFFSETS[1:]], order[1:], first, weights, last=False)
    first_keyed, first_dots = hidden([first_got[NZ // 2]], order[:1], first, weights, carried)

    scale = 1.0 / math.sqrt(all_hidden)
    values = (value_weight, value_right, scale)
    far = partial(first_keyed, first_dots, order[:1], first, *values, parts=2)
    (first_terms,) = partial(first_keyed, first_dots, order[1:], first, *values)
    first_steps = ring_scatter(
        [x[0] for x in far], lambda k: first_terms[OFFSETS.index(k) - 1], NZ, along_z
    )
    step = next(first_steps)
    second_keyed, second_dots = hidden(
        [after(second_all, *step)], jnp.zeros(1, jnp.int32), second, weights
    )
    order = ((my_y + jnp.array((2, 1, -1, 0), jnp.int32)) % NY).astype(jnp.int32)
    (second_terms,) = partial(second_keyed, second_dots, order, second, *values, by_y=True)
    half = second_terms.shape[1] // 2
    second_steps = ring_scatter(
        (second_terms[0, :half], second_terms[0, half:]),
        lambda k: second_terms[(2, 1, -1, 0).index(k)],
        NY,
        along_y,
    )
    step_y = next(second_steps)
    step = first_steps.send(step)
    next_y = second_steps.send(step_y)
    step = first_steps.send(step)
    step, key_update, value_update, _ = barrier((step, key_update, value_update, step_y))
    step = first_steps.send(step)
    second_sum = second_steps.send(next_y)

    def columns(x, index):
        return lax.dynamic_slice_in_dim(x, index * feats, feats, axis=1)

    own_z = lambda k: columns(second_sum, (my_z + k) % NZ)
    own_y = lambda k: columns(first_sum, (my_y + k) % NY)
    second_far = scatter_straight(own_z, (4, 3, -3), along_z)
    first_sum = first_steps.send(after(step, *second_far))
    second_near = scatter_straight(own_z, (2, -2, 1, -1), along_z)
    first_out = total(own_y(0), scatter_straight(own_y, (2, 1, -1), along_y))
    second_out = total(own_z(0), second_far + second_near)
    outputs = jnp.concatenate(
        [x.reshape(TOKS, -1, feats) for x in (first_out, second_out)], axis=1
    )
    outputs = outputs.astype(BF16).transpose(1, 0, 2).reshape(members * TOKS, feats)
    return outputs, key_update.astype(F32), value_update.astype(F32)


def solution(mesh):
    placed = (
        P("pop", "mp"),
        P("mp"),
        P(None, "mp"),
        P("mp", None),
        P("pop", None),
        P("pop", "mp"),
        P("pop", "mp"),
        P("pop", None),
        P("pop"),
    )
    return jax.shard_map(
        shards,
        mesh=mesh,
        in_specs=placed,
        out_specs=(P("pop", "mp"), P("pop", "mp"), P("mp", "pop")),
        check_vma=False,
    )
```

```python
import functools
import math

import jax
import jax.numpy as jnp
from jax import lax
from jax.experimental import pallas as pl
from jax.experimental.pallas import tpu as pltpu
from jax.sharding import PartitionSpec as P

TOKS = 4
NZ = 8
NY = 4
CUT = 10
ALONG_Z = [[z * NY + y for z in range(NZ)] for y in range(NY)]
ALONG_Y = [[z * NY + y for y in range(NY)] for z in range(NZ)]
OFFSETS = (4, 3, -3, 2, -2, 1, -1, 0)
VMEM = 32 * 2**20
F32 = jnp.float32
BF16 = jnp.bfloat16


def along_z(x, step):
    perm = [(z * NY + y, (z + step) % NZ * NY + y) for z in range(NZ) for y in range(NY)]
    return lax.ppermute(x, "mp", perm)


def along_y(x, step):
    perm = [(z * NY + y, z * NY + (y + step) % NY) for z in range(NZ) for y in range(NY)]
    return lax.ppermute(x, "mp", perm)


def after(x, *earlier):
    return lax.optimization_barrier((x, *earlier))[0]


def ring_scatter(far, own, count, move):
    half = far[0].shape[0]
    up, down = yield move(far[0], 1), move(far[1], -1)
    for step in range(count // 2 - 1, 0, -1):
        ahead, behind = own(step).astype(F32), own(-step).astype(F32)
        if step < count // 2 - 1:
            ahead, behind = ahead + up.astype(F32), behind + down.astype(F32)
        else:
            ahead = ahead + jnp.pad(up.astype(F32), ((0, half), (0, 0)))
            behind = behind + jnp.pad(down.astype(F32), ((half, 0), (0, 0)))
        ahead, behind = lax.optimization_barrier((ahead.astype(BF16), behind.astype(BF16)))
        up, down = yield move(ahead, 1), move(behind, -1)
    yield own(0).astype(F32) + up.astype(F32) + down.astype(F32)


def gather_z(x):
    got = {0: x}
    up = down = x
    for step in range(1, NZ // 2):
        up, down = yield along_z(up, 1), along_z(down, -1)
        got[-step], got[step] = up, down
    got[NZ // 2] = along_z(up, 1)
    yield got


def order_kernel(me_ref, *refs):
    *blocks, out = refs
    width = blocks[0].shape[1]
    for k, block in enumerate(blocks):
        place = lax.rem(me_ref[0] + k, NY) * width
        out[:, pl.ds(pl.multiple_of(place, width), width)] = block[...]


def in_order(blocks, me):
    rows, width = blocks[0].shape
    return pl.pallas_call(
        order_kernel,
        in_specs=[pl.BlockSpec(memory_space=pltpu.SMEM)]
        + [pl.BlockSpec(memory_space=pltpu.VMEM)] * NY,
        out_specs=pl.BlockSpec(memory_space=pltpu.VMEM),
        out_shape=jax.ShapeDtypeStruct((rows, NY * width), BF16),
        cost_estimate=pl.CostEstimate(
            flops=0, bytes_accessed=4 * NY * rows * width, transcendentals=0
        ),
        name="in_order",
    )(me.reshape(1).astype(jnp.int32), *blocks)


def scatter_straight(own, offsets, move):
    return [move(own(k).astype(BF16), k) for k in offsets]


def total(own, sent):
    return sum((x.astype(F32) for x in sent), own)


def dot(a, b):
    return jnp.dot(a, b, preferred_element_type=F32)


def total_over_pop(x):
    for bit in (1, 2, 4):
        x = x + lax.ppermute(x, "pop", [(i, i ^ bit) for i in range(8)])
    return x


def columns(ref, first, step, count, width):
    parts = [
        ref[:, pl.ds(pl.multiple_of((first + step * n) * width, width), width)]
        for n in range(count)
    ]
    return jnp.concatenate(parts, axis=1)


def sums_kernel(members, carried, order_ref, *refs):
    *blocks, weight, left, base_ref, products_ref = refs
    base = products = 0.0
    if carried:
        *blocks, base_in, products_in = blocks
        base, products = base_in[...], products_in[...]
    lanes = products_ref.shape[1]
    for n, block in enumerate(blocks):
        if len(block.shape) == 2:
            tokens = block[...]
        else:
            tokens = jnp.concatenate(
                [block[y, z] for z in range(NZ) for y in range(NY)], axis=1
            )
        deep = tokens.shape[1]
        place = pl.ds(0, deep)
        if len(blocks) > 1:
            place = pl.ds(pl.multiple_of(order_ref[n] * deep, deep), deep)
        base = base + dot(tokens, weight[place, :])
        terms = tokens.astype(F32) * left[members, place].astype(F32)
        products = products + sum(terms[:, at : at + lanes] for at in range(0, deep, lanes))
    base_ref[...] = base
    products_ref[...] = products


def hidden_kernel(scale, members, carried, order_ref, *refs):
    *given, right, value_left, keyed_ref, value_dots_ref, base, products = refs
    sums_kernel(members, carried, order_ref, *given, base, products)
    left_dots = jnp.sum(products[...], axis=1, keepdims=True)
    hidden = base[...] + left_dots * (right[members, :].astype(F32) * scale)
    hidden = jnp.maximum(hidden, 0.0)
    keyed = (hidden * hidden).astype(BF16)
    keyed_ref[...] = keyed
    sums = jnp.sum(keyed.astype(F32) * value_left[members, :].astype(F32), axis=1, keepdims=True)
    value_dots_ref[...] = jnp.broadcast_to(sums, value_dots_ref.shape)


def hidden(blocks, order, members, weights, carried=(), last=True):
    key_weight, key_left, key_right, value_left = weights
    count = members.stop - members.start
    units = key_weight.shape[1]
    rows, deep = count * TOKS, blocks[0].shape[-1]
    whole = lambda x: pl.BlockSpec(x.shape, lambda i, order: (0, 0))
    part = lambda wide: pl.BlockSpec((count, wide), lambda i, order: (i, 0))
    if len(blocks[0].shape) == 2:
        specs = [part(deep) for _ in blocks]
    else:
        specs = [pl.BlockSpec((NY, NZ, count, deep), lambda i, order: (0, 0, i, 0))]
        deep = deep * NY * NZ
    specs += [part(x.shape[1]) for x in carried]
    if len(blocks) > 1:
        specs += [whole(key_weight), whole(key_left)]
    else:
        specs += [
            pl.BlockSpec((deep, units), lambda i, order: (order[0], 0)),
            pl.BlockSpec((key_left.shape[0], deep), lambda i, order: (0, order[0])),
        ]
    given = [*blocks, *carried, key_weight, key_left]
    if last:
        kernel = functools.partial(
            hidden_kernel, 1.0 / math.sqrt(key_left.shape[1]), members, bool(carried)
        )
        given, specs = given + [key_right, value_left], specs + [whole(key_right), whole(value_left)]
        scratch = [pltpu.VMEM((count, units), F32), pltpu.VMEM((count, 128), F32)]
    else:
        kernel = functools.partial(sums_kernel, members, bool(carried))
        scratch = []
    features = deep * len(blocks)
    return pl.pallas_call(
        kernel,
        grid_spec=pltpu.PrefetchScalarGridSpec(
            num_scalar_prefetch=1,
            grid=(TOKS,),
            in_specs=specs,
            out_specs=[part(units), part(128)],
            scratch_shapes=scratch,
        ),
        out_shape=[
            jax.ShapeDtypeStruct((rows, units), BF16 if last else F32),
            jax.ShapeDtypeStruct((rows, 128), F32),
        ],
        compiler_params=pltpu.CompilerParams(vmem_limit_bytes=VMEM),
        cost_estimate=pl.CostEstimate(
            flops=2 * rows * features * units,
            bytes_accessed=2 * features * (rows + units + key_left.shape[0]) + 4 * rows * units,
            transcendentals=0,
        ),
        name="hidden",
    )(order, *given)


def partial_terms(keyed, value_dots, weight, rights, scale):
    terms = dot(keyed[...], weight)
    rights = rights.astype(F32) * scale
    count = rights.shape[0]
    parts = []
    for token in range(TOKS):
        rows = slice(token * count, (token + 1) * count)
        parts.append((terms[rows] + value_dots[rows, :1] * rights).astype(BF16))
    return parts


def partial_z_kernel(scale, members, order_ref, keyed, value_dots, weight, right, *outs):
    count = members.stop - members.start
    parts = partial_terms(keyed, value_dots, weight[...], right[members, :], scale)
    for token, part in enumerate(parts):
        out = outs[token * len(outs) // TOKS]
        at = token % (TOKS // len(outs)) * count
        out[0, at : at + count, :] = part


def partial_y_kernel(scale, members, order_ref, keyed, value_dots, weight, right, out):
    y = order_ref[pl.program_id(0)]
    count = members.stop - members.start
    feats = out.shape[2] // NZ
    picks = [
        pl.ds(pl.multiple_of((z * NY + y) * feats, feats), feats) for z in range(NZ)
    ]
    weights = jnp.concatenate([weight[:, pick] for pick in picks], axis=1)
    rights = jnp.concatenate([right[members, pick] for pick in picks], axis=1)
    parts = partial_terms(keyed, value_dots, weights, rights, scale)
    for token, part in enumerate(parts):
        out[0, token * count : (token + 1) * count, :] = part


def partial(keyed, value_dots, order, members, weight, right, scale, by_y=False, parts=1):
    rows, units = keyed.shape
    width = weight.shape[1]
    whole = lambda x: pl.BlockSpec(x.shape, lambda i, order: (0, 0))
    ring = NY if by_y else NZ
    if by_y:
        kernel = partial_y_kernel
        weight_specs = [whole(weight), whole(right)]
    else:
        kernel = partial_z_kernel
        weight_specs = [
            pl.BlockSpec((x.shape[0], width // NZ), lambda i, order: (0, order[i]))
            for x in (weight, right)
        ]
    shape = (len(order), rows // parts, width // ring)
    return pl.pallas_call(
        functools.partial(kernel, scale, members),
        grid_spec=pltpu.PrefetchScalarGridSpec(
            num_scalar_prefetch=1,
            grid=(len(order),),
            in_specs=[whole(keyed), whole(value_dots)] + weight_specs,
            out_specs=[pl.BlockSpec((1,) + shape[1:], lambda i, order: (i, 0, 0))] * parts,
        ),
        out_shape=[jax.ShapeDtypeStruct(shape, BF16)] * parts,
        compiler_params=pltpu.CompilerParams(vmem_limit_bytes=VMEM),
        cost_estimate=pl.CostEstimate(
            flops=2 * rows * units * len(order) * (width // ring),
            bytes_accessed=2 * len(order) * (width // ring) * (rows + units),
            transcendentals=0,
        ),
        name="partial",
    )(order, keyed, value_dots, weight, right)


def shards(
    inputs,
    mix_gain,
    key_weight,
    value_weight,
    key_left,
    key_right,
    value_left,
    value_right,
    fitness,
):
    members, width = key_left.shape
    feats = inputs.shape[1]
    hidden_units = key_weight.shape[1]
    all_members = members * lax.axis_size("pop")
    all_hidden = hidden_units * lax.axis_size("mp")
    member_scale = math.sqrt(all_members)
    me = lax.axis_index("mp")
    my_z, my_y = me // NY, me % NY
    tokens = inputs.reshape(members, TOKS, feats).transpose(1, 0, 2).astype(F32)
    previous = jnp.concatenate([jnp.zeros_like(tokens[:1]), tokens[:-1]], axis=0)
    shifted = (tokens + mix_gain * (previous - tokens)).astype(BF16)
    barrier = lax.optimization_barrier
    cut = members * CUT // 16
    first, second = slice(0, cut), slice(cut, members)
    latter = shifted[:, members // 2 :].reshape(-1, feats)
    second_z = lax.all_gather(latter, "mp", axis_index_groups=ALONG_Z)
    mine = shifted[:, first].reshape(-1, feats)
    first_block = in_order([mine] + [along_y(mine, -k) for k in (1, 2, 3)], my_y)
    steps = gather_z(first_block)
    step = next(steps)

    pair = after(fitness, first_block).reshape(1, members)
    pair = jnp.concatenate([pair, pair * pair], axis=0)
    sums = total_over_pop(jnp.sum(pair, axis=1, keepdims=True)) / all_members
    mean, square = sums[:1], sums[1:]
    scores = (fitness.reshape(1, members) - mean) / jnp.sqrt(square - mean * mean + 1e-05)
    scores = scores.reshape(members)

    step, scores = barrier((step, scores))
    step = steps.send(step)

    scaled_right = (scores[:, None] * key_right.astype(F32)).astype(BF16)
    scaled_value = (scores[:, None] * value_right.astype(F32)).astype(BF16)
    member_dims = (((0,), (0,)), ((), ()))
    key_terms = lax.dot_general(
        key_left, scaled_right, member_dims, preferred_element_type=F32
    )
    value_terms = lax.dot_general(
        value_left, scaled_value, member_dims, preferred_element_type=F32
    )
    key_terms = (key_terms / member_scale).astype(BF16)
    value_terms = (value_terms / member_scale).astype(BF16)

    step, key_terms, value_terms = barrier((step, key_terms, value_terms))
    second_z = after(second_z, *step).reshape(NZ, TOKS, -1, feats)[:, :, cut - members // 2 :]
    second_all = lax.all_gather(
        second_z.reshape(NZ, -1, feats), "mp", axis_index_groups=ALONG_Y
    )
    step = barrier(steps.send(step))
    first_got = steps.send(step)
    order = ((my_z + jnp.array(OFFSETS, jnp.int32)) % NZ).astype(jnp.int32)
    key_update = lax.psum_scatter(key_terms, "pop", scatter_dimension=0, tiled=True)
    value_update = lax.psum_scatter(value_terms, "pop", scatter_dimension=1, tiled=True)

    weights = (key_weight, key_left, key_right, value_left)
    carried = hidden([first_got[k] for k in OFFSETS[1:]], order[1:], first, weights, last=False)
    first_keyed, first_dots = hidden([first_got[NZ // 2]], order[:1], first, weights, carried)

    scale = 1.0 / math.sqrt(all_hidden)
    values = (value_weight, value_right, scale)
    far = partial(first_keyed, first_dots, order[:1], first, *values, parts=2)
    (first_terms,) = partial(first_keyed, first_dots, order[1:], first, *values)
    first_steps = ring_scatter(
        [x[0] for x in far], lambda k: first_terms[OFFSETS.index(k) - 1], NZ, along_z
    )
    step = barrier(next(first_steps))
    second_keyed, second_dots = hidden(
        [after(second_all, *step)], jnp.zeros(1, jnp.int32), second, weights
    )
    order = ((my_y + jnp.array((2, 1, -1, 0), jnp.int32)) % NY).astype(jnp.int32)
    (second_terms,) = partial(second_keyed, second_dots, order, second, *values, by_y=True)
    half = second_terms.shape[1] // 2
    second_steps = ring_scatter(
        (second_terms[0, :half], second_terms[0, half:]),
        lambda k: second_terms[(2, 1, -1, 0).index(k)],
        NY,
        along_y,
    )
    step_y = next(second_steps)
    step = first_steps.send(step)
    next_y = second_steps.send(after(step_y, *step))
    step = first_steps.send(step)
    step, key_update, value_update = barrier((step, key_update, value_update))
    step = first_steps.send(step)
    second_sum = second_steps.send(next_y)

    def columns(x, index):
        return lax.dynamic_slice_in_dim(x, index * feats, feats, axis=1)

    own_z = lambda k: columns(second_sum, (my_z + k) % NZ)
    own_y = lambda k: columns(first_sum, (my_y + k) % NY)
    second_far = scatter_straight(own_z, (4, 3, -3), along_z)
    second_near = scatter_straight(own_z, (2, -2, 1, -1), along_z)
    first_sum = first_steps.send(after(step, *second_far, *second_near))
    first_out = total(own_y(0), scatter_straight(own_y, (2, 1, -1), along_y))
    second_out = total(own_z(0), second_far + second_near)
    outputs = jnp.concatenate(
        [x.reshape(TOKS, -1, feats) for x in (first_out, second_out)], axis=1
    )
    outputs = outputs.astype(BF16).transpose(1, 0, 2).reshape(members * TOKS, feats)
    return outputs, key_update.astype(F32), value_update.astype(F32)


def solution(mesh):
    placed = (
        P("pop", "mp"),
        P("mp"),
        P(None, "mp"),
        P("mp", None),
        P("pop", None),
        P("pop", "mp"),
        P("pop", "mp"),
        P("pop", None),
        P("pop"),
    )
    return jax.shard_map(
        shards,
        mesh=mesh,
        in_specs=placed,
        out_specs=(P("pop", "mp"), P("pop", "mp"), P("mp", "pop")),
        check_vma=False,
    )
```
